32 devices in a mesh: ctx: 32 (over z, y, x, core), tp: 1.
Axes of the slice: x: 2, y: 2, z: 4, core: 2. Of those that a mesh axis runs over, the one named last changes fastest.
Arguments:
- queries: bfloat16 [4096, 8192], P('ctx', 'tp'), may hold values from -32 to 32
- key_proj: bfloat16 [4096, 1024], P('ctx', 'tp'), may hold values from -12.5 to 12.5
- value_proj: bfloat16 [4096, 1024], P('ctx', 'tp'), may hold values from -6 to 6
- grad_out: bfloat16 [4096, 8192], P('ctx', 'tp'), may hold values from -6 to 6
- key_weight: bfloat16 [8192, 1024], P(None, 'tp'), may hold values from -0.1875 to 0.1875
- value_weight: bfloat16 [8192, 1024], P(None, 'tp'), may hold values from -0.1875 to 0.1875
- doc_start: int32 [4096], P('ctx'), may hold values from 0 to 4095, as said below
Outputs:
- grad_query: bfloat16 [4096, 8192], P('ctx', 'tp')
- grad_key: bfloat16 [4096, 1024], P('ctx', 'tp')
- grad_value: bfloat16 [4096, 1024], P('ctx', 'tp')
- grad_input: bfloat16 [4096, 8192], P('ctx', 'tp')
The draws below stay inside these ranges and needn't reach their ends.
Inputs may be any that keep to these rules, and one draw needn't show every extreme that they name: doc_start[p] is the first position of the document holding p; documents are runs of consecutive positions, each of 1 to 2048 positions; the first document has exactly 2048 positions and the last position is a document of its own.
All inputs are finite; a program needn't handle non-finite values.
Results may differ from the reference program's by a relative error of at most 0.034.
Values may be sent and summed in bfloat16 or wider, within the bound.
A program may use at most 128 MiB of HBM per device.

```python
import math
import jax
import jax.numpy as jnp
from jax import lax

D = 8192
HEADS = 64
KV_HEADS = 8
HD = 128
TOK_DEV = 128
DOC_MOST = 2048
TOKENS = 4096
REACH = 16


def shared_keys(key):
    base_keys = jax.random.normal(jax.random.fold_in(key, 11), (TOKENS, KV_HEADS * HD), jnp.float32)
    base_keys = jnp.clip(base_keys, -4.0, 4.0)
    return base_keys


def draw_key_proj(key, part):
    return shared_keys(key).astype(jnp.bfloat16)


def draw_queries(key, part):
    drawn = jnp.clip(jax.random.normal(jax.random.fold_in(key, 23), (TOKENS, HEADS * HD), jnp.float32), -4.0, 4.0)
    return drawn.astype(jnp.bfloat16)


def draw_doc_start(key, part):
    lengths = jax.random.randint(jax.random.fold_in(key, 5), (TOKENS,), 1, DOC_MOST + 1)
    lengths = jnp.where(jnp.arange(TOKENS) == 0, DOC_MOST, lengths).astype(jnp.int32)
    ends = jnp.cumsum(lengths).astype(jnp.int32)
    starts = ends - lengths
    positions = jnp.arange(TOKENS, dtype=jnp.int32)
    doc_index = jnp.searchsorted(ends, positions, side='right')
    first = starts[doc_index].astype(jnp.int32)
    return jnp.where(positions == TOKENS - 1, TOKENS - 1, first).astype(jnp.int32)


def levels(rng, dims, split, smallest, top_value):
    loudness, own = 1.0, jax.random.fold_in(rng, 6)
    for position, shards_of in split:
        heights = jnp.exp(jax.random.uniform(jax.random.fold_in(own, position), (shards_of,), jnp.float32, smallest / len(split), top_value / len(split)))
        loudness = loudness * jnp.repeat(heights, dims[position] // shards_of).reshape([-1 if axis == position else 1 for axis in range(len(dims))])
    return loudness


def normal_values(key, extent, spread, most, cuts=(), kind=jnp.bfloat16):
    values = jax.random.normal(key, extent, jnp.float32) * spread
    if len(cuts) > 0:
        values = levels(key, extent, cuts, -0.22, 0.18) * values
    return jnp.clip(values, min=-most, max=most).astype(kind)


def setup_inputs(seed: int = 0) -> dict:
    keys = jax.random.split(jax.random.key(seed), 8)
    queries = draw_queries(jax.random.fold_in(keys[7], 71), 0)
    key_proj = draw_key_proj(jax.random.fold_in(keys[7], 71), 0)
    value_proj = normal_values(keys[2], (TOKENS, KV_HEADS * HD), 1.0, 6.0, ((0, 32),))
    grad_out = normal_values(keys[3], (TOKENS, HEADS * HD), 1.0, 6.0, ((0, 32),))
    key_weight = normal_values(keys[4], (D, KV_HEADS * HD), (KV_HEADS * HD) ** -0.5, 0.1875)
    value_weight = normal_values(keys[5], (D, KV_HEADS * HD), (KV_HEADS * HD) ** -0.5, 0.1875)
    doc_start = draw_doc_start(jax.random.fold_in(keys[7], 71), 0)
    return {"queries": queries, "key_proj": key_proj, "value_proj": value_proj, "grad_out": grad_out, "key_weight": key_weight, "value_weight": value_weight, "doc_start": doc_start}


def rounded(values):
    return lax.optimization_barrier(values.astype(jnp.bfloat16)).astype(jnp.float32)

def reference(queries, key_proj, value_proj, grad_out, key_weight, value_weight, doc_start):
    group_size = HEADS // KV_HEADS
    soft_scale = 1.0 / math.sqrt(HD)
    window = (REACH + 1) * TOK_DEV
    blocks = TOKENS // TOK_DEV

    def one_block(loop_carry, blk_index):
        grad_keys, grad_values = loop_carry
        query_start = (blk_index * TOK_DEV).astype(jnp.int32)
        key_start = (jnp.maximum(blk_index - REACH, 0) * TOK_DEV).astype(jnp.int32)
        query_rows = lax.dynamic_slice_in_dim(queries, query_start, TOK_DEV, 0).astype(jnp.float32)
        query_rows = query_rows.reshape(TOK_DEV, KV_HEADS, group_size, HD)
        cot_rows = lax.dynamic_slice_in_dim(grad_out, query_start, TOK_DEV, 0).astype(jnp.float32)
        cot_rows = cot_rows.reshape(TOK_DEV, KV_HEADS, group_size, HD)
        key_rows = lax.dynamic_slice_in_dim(key_proj, key_start, window, 0).astype(jnp.float32).reshape(window, KV_HEADS, HD)
        value_rows = lax.dynamic_slice_in_dim(value_proj, key_start, window, 0).astype(jnp.float32).reshape(window, KV_HEADS, HD)
        query_pos = query_start + jnp.arange(TOK_DEV, dtype=jnp.int32)
        key_pos = key_start + jnp.arange(window, dtype=jnp.int32)
        first_pos = lax.dynamic_slice_in_dim(doc_start, query_start, TOK_DEV, 0)
        visible = (key_pos[None, :] <= query_pos[:, None]) & (key_pos[None, :] >= first_pos[:, None])
        scores = jnp.einsum('qkgd,pkd->kgqp', query_rows, key_rows) * soft_scale
        scores = jnp.where(visible, scores, -jnp.inf)
        rowmax = lax.optimization_barrier(jnp.max(scores, axis=-1, keepdims=True))
        expw = jnp.exp(scores - rowmax)
        row_total = lax.optimization_barrier(jnp.sum(expw, axis=-1, keepdims=True))
        attn_out = jnp.einsum('kgqp,pkd->kgqd', rounded(expw), value_rows) / row_total
        attn_out = rounded(attn_out)
        log_total = rowmax + jnp.log(row_total)
        delta = jnp.einsum('qkgd,kgqd->kgq', cot_rows, attn_out)[..., None]
        probs = jnp.exp(scores - log_total)
        grad_probs = jnp.einsum('qkgd,pkd->kgqp', cot_rows, value_rows)
        grad_scores = rounded(probs * (grad_probs - delta))
        grad_q = jnp.einsum('kgqp,pkd->qkgd', grad_scores, key_rows) * soft_scale
        key_part = jnp.einsum('kgqp,qkgd->pkd', grad_scores, query_rows) * soft_scale
        value_part = jnp.einsum('kgqp,qkgd->pkd', rounded(probs), cot_rows)
        old_keys = lax.dynamic_slice_in_dim(grad_keys, key_start, window, 0)
        old_values = lax.dynamic_slice_in_dim(grad_values, key_start, window, 0)
        grad_keys = lax.dynamic_update_slice_in_dim(grad_keys, old_keys + key_part.reshape(window, KV_HEADS * HD), key_start, 0)
        grad_values = lax.dynamic_update_slice_in_dim(grad_values, old_values + value_part.reshape(window, KV_HEADS * HD), key_start, 0)
        return ((grad_keys, grad_values), grad_q.reshape(TOK_DEV, HEADS * HD).astype(jnp.bfloat16))
    zeros_kv = jnp.zeros((TOKENS, KV_HEADS * HD), jnp.float32)
    (grad_keys, grad_values), grad_blocks = lax.scan(one_block, (zeros_kv, zeros_kv), jnp.arange(blocks, dtype=jnp.int32))
    grad_query = grad_blocks.reshape(TOKENS, HEADS * HD)
    grad_key = grad_keys.astype(jnp.bfloat16)
    grad_value = grad_values.astype(jnp.bfloat16)
    grad_input = jnp.einsum('tc,dc->td', grad_key.astype(jnp.float32), key_weight.astype(jnp.float32))
    grad_input = grad_input + jnp.einsum('tc,dc->td', grad_value.astype(jnp.float32), value_weight.astype(jnp.float32))
    return (grad_query, grad_key, grad_value, grad_input.astype(jnp.bfloat16))
```

```python
import functools
import math

import jax
import jax.numpy as jnp
from jax import lax
from jax.experimental import pallas as pl
from jax.experimental.pallas import tpu as pltpu
from jax.sharding import PartitionSpec as P

HEADS = 64
KV_HEADS = 8
HD = 128
GROUP = HEADS // KV_HEADS
DOC_MOST = 2048
TILE = 256
CHUNKS = 4

NEGATIVE = -1e30
NT = (((1,), (1,)), ((), ()))


def attention_kernel(
    tok_rows, key_tiles, marks, pos_ref, first_ref, query_ref, cot_ref, kv_ref, dq_ref, dkv_ref,
    query_rows, cot_rows, score_ref, weight_ref, dqt_ref,
):
    rows = GROUP * tok_rows
    soft_scale = 1.0 / math.sqrt(HD)
    exp2_scale = soft_scale * math.log2(math.e)
    low, full_low, full_high, high = marks[0], marks[1], marks[2], marks[3]

    for head in range(GROUP):
        query_rows[head * tok_rows:(head + 1) * tok_rows, :] = query_ref[:, head * HD:(head + 1) * HD]
        cot_rows[head * tok_rows:(head + 1) * tok_rows, :] = cot_ref[:, head * HD:(head + 1) * HD]

    def fold(values):
        return values.reshape(TILE // 8, 8, rows)

    def at(tile):
        return pl.ds(pl.multiple_of(tile * TILE, TILE), TILE)

    def slot(tile):
        return pl.ds(pl.multiple_of((tile - low) * TILE, TILE), TILE)

    def score_step(masked, tile, rowmax):
        scores = lax.dot_general(
            kv_ref[at(tile), :HD], query_rows[...], NT, preferred_element_type=jnp.float32
        )
        if masked:
            key_pos = tile * TILE + lax.broadcasted_iota(jnp.int32, (TILE, rows), 0)
            visible = (key_pos <= pos_ref[...]) & (key_pos >= first_ref[...])
            scores = jnp.where(visible, scores, NEGATIVE)
        score_ref[slot(tile), :] = scores
        return jnp.maximum(rowmax, jnp.max(fold(scores), axis=0))

    rowmax = jnp.full((8, rows), NEGATIVE, jnp.float32)
    rowmax = lax.fori_loop(low, full_low, functools.partial(score_step, True), rowmax)
    rowmax = lax.fori_loop(full_low, full_high, functools.partial(score_step, False), rowmax)
    rowmax = lax.fori_loop(full_high, high, functools.partial(score_step, True), rowmax)
    shift = jnp.max(rowmax, axis=0, keepdims=True) * exp2_scale

    def weight_step(tile, sums):
        total, dot_sum = sums
        weights = jnp.exp2(score_ref[slot(tile), :] * exp2_scale - shift)
        grad_probs = lax.dot_general(
            kv_ref[at(tile), HD:], cot_rows[...], NT, preferred_element_type=jnp.float32
        )
        weight_ref[slot(tile), :] = weights.astype(jnp.bfloat16)
        score_ref[slot(tile), :] = grad_probs
        total = total + jnp.sum(fold(weights), axis=0)
        dot_sum = dot_sum + jnp.sum(fold(weights * grad_probs), axis=0)
        return (total, dot_sum)

    zeros = jnp.zeros((8, rows), jnp.float32)
    total, dot_sum = lax.fori_loop(low, high, weight_step, (zeros, zeros))
    inverse = 1.0 / jnp.sum(total, axis=0, keepdims=True)
    delta = jnp.sum(dot_sum, axis=0, keepdims=True) * inverse

    for head in range(GROUP):
        part = slice(head * tok_rows, (head + 1) * tok_rows)
        scale = jnp.broadcast_to(inverse[:, part], (HD, tok_rows)).T
        query_rows[part, :] = (query_rows[part, :].astype(jnp.float32) * (scale * soft_scale)).astype(jnp.bfloat16)
        cot_rows[part, :] = (cot_rows[part, :].astype(jnp.float32) * scale).astype(jnp.bfloat16)

    dqt_ref[...] = jnp.zeros_like(dqt_ref)

    def grad_step(tile, nothing):
        weights = weight_ref[slot(tile), :]
        grad_scores = (
            weights.astype(jnp.float32) * (score_ref[slot(tile), :] - delta)
        ).astype(jnp.bfloat16)
        dkv_ref[at(tile), HD:] = jnp.dot(
            weights, cot_rows[...], preferred_element_type=jnp.float32
        ).astype(jnp.bfloat16)
        dkv_ref[at(tile), :HD] = jnp.dot(
            grad_scores, query_rows[...], preferred_element_type=jnp.float32
        ).astype(jnp.bfloat16)
        dqt_ref[...] += jnp.dot(
            kv_ref[at(tile), :HD].T, grad_scores, preferred_element_type=jnp.float32
        )
        return nothing

    lax.fori_loop(low, high, grad_step, 0)

    def clear(tile, nothing):
        dkv_ref[at(tile), :] = jnp.zeros((TILE, 2 * HD), jnp.bfloat16)
        return nothing

    lax.fori_loop(0, low, clear, 0)
    lax.fori_loop(high, key_tiles, clear, 0)

    out_scale = inverse * soft_scale
    for head in range(GROUP):
        part = slice(head * tok_rows, (head + 1) * tok_rows)
        dq_ref[:, head * HD:(head + 1) * HD] = (dqt_ref[:, part] * out_scale[:, part]).T.astype(jnp.bfloat16)


def attention(marks, pos, first, queries, grad_out, kv, tok_rows, first_head, heads_here):
    rows = GROUP * tok_rows
    keys = kv.shape[0]
    slots = (DOC_MOST + tok_rows + 2 * TILE - 2) // TILE * TILE
    wide = GROUP * HD
    flops = heads_here * 5 * 2 * rows * (DOC_MOST // 2) * HD
    return pl.pallas_call(
        functools.partial(attention_kernel, tok_rows, keys // TILE),
        grid_spec=pltpu.PrefetchScalarGridSpec(
            num_scalar_prefetch=1,
            grid=(heads_here,),
            in_specs=[
                pl.BlockSpec((1, rows), lambda h, marks: (0, 0)),
                pl.BlockSpec((1, rows), lambda h, marks: (0, 0)),
                pl.BlockSpec((tok_rows, wide), lambda h, marks: (0, first_head + h)),
                pl.BlockSpec((tok_rows, wide), lambda h, marks: (0, first_head + h)),
                pl.BlockSpec((keys, 2 * HD), lambda h, marks: (0, h)),
            ],
            out_specs=[
                pl.BlockSpec((tok_rows, wide), lambda h, marks: (0, h)),
                pl.BlockSpec((keys, 2 * HD), lambda h, marks: (0, h)),
            ],
            scratch_shapes=[
                pltpu.VMEM((rows, HD), jnp.bfloat16),
                pltpu.VMEM((rows, HD), jnp.bfloat16),
                pltpu.VMEM((slots, rows), jnp.float32),
                pltpu.VMEM((slots, rows), jnp.bfloat16),
                pltpu.VMEM((HD, rows), jnp.float32),
            ],
        ),
        out_shape=[
            jax.ShapeDtypeStruct((tok_rows, heads_here * wide), jnp.bfloat16),
            jax.ShapeDtypeStruct((keys, heads_here * 2 * HD), jnp.bfloat16),
        ],
        compiler_params=pltpu.CompilerParams(
            dimension_semantics=("arbitrary",), vmem_limit_bytes=48 * 1024 * 1024
        ),
        cost_estimate=pl.CostEstimate(flops=flops * 4, bytes_accessed=heads_here * 4 * 1024 * 1024, transcendentals=0),
    )(marks, pos, first, queries, grad_out, kv)


def shards(queries, key_proj, value_proj, grad_out, key_weight, value_weight, doc_start):
    tok_rows = queries.shape[0]
    heads_kv = key_proj.shape[1] // HD
    my_index = lax.axis_index("ctx")
    begin = my_index * tok_rows
    low = doc_start[0] // TILE
    full_low = (doc_start[tok_rows - 1] + TILE - 1) // TILE
    full_high = (begin + 1) // TILE
    high = (begin + tok_rows + TILE - 1) // TILE
    full_low = jnp.minimum(full_low, high)
    full_high = jnp.maximum(full_high, full_low)
    marks = jnp.stack([low, full_low, full_high, high]).astype(jnp.int32)
    pos = jnp.tile(begin + jnp.arange(tok_rows, dtype=jnp.int32), GROUP)[None]
    first = jnp.tile(doc_start, GROUP)[None]

    chunks = min(CHUNKS, heads_kv)
    per = heads_kv // chunks
    pair = jnp.stack(
        [key_proj.reshape(tok_rows, heads_kv, HD), value_proj.reshape(tok_rows, heads_kv, HD)], axis=2
    ).reshape(tok_rows, heads_kv * 2 * HD)
    grad_queries, sums = [], []
    for chunk in range(chunks):
        part = pair[:, chunk * per * 2 * HD:(chunk + 1) * per * 2 * HD]
        kv = lax.all_gather(part, "ctx", tiled=True)
        dq, dkv = attention(marks, pos, first, queries, grad_out, kv, tok_rows, chunk * per, per)
        grad_queries.append(dq)
        sums.append(lax.psum_scatter(dkv, "ctx", scatter_dimension=0, tiled=True))
    grad_query = jnp.concatenate(grad_queries, axis=1)
    both = jnp.concatenate(sums, axis=1).reshape(tok_rows, heads_kv, 2, HD)
    grad_key = both[:, :, 0].reshape(tok_rows, heads_kv * HD)
    grad_value = both[:, :, 1].reshape(tok_rows, heads_kv * HD)
    partial_input = jnp.einsum(
        "rc,dc->rd", grad_key, key_weight, preferred_element_type=jnp.float32
    )
    partial_input = partial_input + jnp.einsum(
        "rc,dc->rd", grad_value, value_weight, preferred_element_type=jnp.float32
    )
    grad_input = lax.psum_scatter(
        partial_input.astype(jnp.bfloat16), "tp", scatter_dimension=1, tiled=True
    )
    return (grad_query, grad_key, grad_value, grad_input)


def solution(mesh):
    in_specs = (
        P("ctx", "tp"),
        P("ctx", "tp"),
        P("ctx", "tp"),
        P("ctx", "tp"),
        P(None, "tp"),
        P(None, "tp"),
        P("ctx"),
    )
    out_specs = (P("ctx", "tp"), P("ctx", "tp"), P("ctx", "tp"), P("ctx", "tp"))
    return jax.shard_map(shards, mesh=mesh, in_specs=in_specs, out_specs=out_specs, check_vma=False)
```

```python
import functools
import math

import jax
import jax.numpy as jnp
from jax import lax
from jax.experimental import pallas as pl
from jax.experimental.pallas import tpu as pltpu
from jax.sharding import PartitionSpec as P

HEADS = 64
KV_HEADS = 8
HD = 128
GROUP = HEADS // KV_HEADS
DOC_MOST = 2048
TILE = 256
CHUNKS = 4
PLANE = 8
BACK = 2

NEGATIVE = -1e30
NT = (((1,), (1,)), ((), ()))


def attention_kernel(
    tok_rows, key_tiles, marks, pos_ref, first_ref, query_ref, cot_ref, own_in, y_in, x_in, core_in,
    dq_ref, own_out, y_out, x_out, core_out,
    query_rows, cot_rows, score_ref, weight_ref, dqt_ref, kv_ref, dkv_ref,
):
    rows = GROUP * tok_rows
    soft_scale = 1.0 / math.sqrt(HD)
    exp2_scale = soft_scale * math.log2(math.e)
    low, full_low, full_high, high = marks[0], marks[1], marks[2], marks[3]
    base, place = marks[4], marks[5]

    blocks = [(own_in, own_out, plane, plane * PLANE + place) for plane in range(BACK + 1)]
    for piece_in, piece_out, offsets in (
        (y_in, y_out, (4,)), (x_in, x_out, (2, 6)), (core_in, core_out, (1, 5, 3, 7))
    ):
        for number, offset in enumerate(offsets):
            source = place ^ offset
            first_plane = jnp.where(source > place, 0, 1)
            for plane in range(BACK):
                blocks.append(
                    (piece_in, piece_out, number * BACK + plane, (first_plane + plane) * PLANE + source)
                )

    def block_at(index):
        return pl.ds(pl.multiple_of(index * tok_rows, tok_rows), tok_rows)

    @pl.when(pl.program_id(0) == 0)
    def _():
        kv_ref[...] = jnp.zeros_like(kv_ref)

    for piece_in, _, number, index in blocks:
        kv_ref[block_at(index), :] = piece_in[number]

    for head in range(GROUP):
        query_rows[head * tok_rows:(head + 1) * tok_rows, :] = query_ref[:, head * HD:(head + 1) * HD]
        cot_rows[head * tok_rows:(head + 1) * tok_rows, :] = cot_ref[:, head * HD:(head + 1) * HD]

    def fold(values):
        return values.reshape(TILE // 8, 8, rows)

    def at(tile):
        return pl.ds(pl.multiple_of(tile * TILE, TILE), TILE)

    def slot(tile):
        return pl.ds(pl.multiple_of((tile - low) * TILE, TILE), TILE)

    def score_step(masked, tile, rowmax):
        scores = lax.dot_general(
            kv_ref[at(tile), :HD], query_rows[...], NT, preferred_element_type=jnp.float32
        )
        if masked:
            key_pos = (base + tile) * TILE + lax.broadcasted_iota(jnp.int32, (TILE, rows), 0)
            visible = (key_pos <= pos_ref[...]) & (key_pos >= first_ref[...])
            scores = jnp.where(visible, scores, NEGATIVE)
        score_ref[slot(tile), :] = scores
        return jnp.maximum(rowmax, jnp.max(fold(scores), axis=0))

    rowmax = jnp.full((8, rows), NEGATIVE, jnp.float32)
    rowmax = lax.fori_loop(low, full_low, functools.partial(score_step, True), rowmax)
    rowmax = lax.fori_loop(full_low, full_high, functools.partial(score_step, False), rowmax)
    rowmax = lax.fori_loop(full_high, high, functools.partial(score_step, True), rowmax)
    shift = jnp.max(rowmax, axis=0, keepdims=True) * exp2_scale

    def weight_step(tile, sums):
        total, dot_sum = sums
        weights = jnp.exp2(score_ref[slot(tile), :] * exp2_scale - shift)
        grad_probs = lax.dot_general(
            kv_ref[at(tile), HD:], cot_rows[...], NT, preferred_element_type=jnp.float32
        )
        weight_ref[slot(tile), :] = weights.astype(jnp.bfloat16)
        score_ref[slot(tile), :] = grad_probs
        total = total + jnp.sum(fold(weights), axis=0)
        dot_sum = dot_sum + jnp.sum(fold(weights * grad_probs), axis=0)
        return (total, dot_sum)

    zeros = jnp.zeros((8, rows), jnp.float32)
    total, dot_sum = lax.fori_loop(low, high, weight_step, (zeros, zeros))
    inverse = 1.0 / jnp.sum(total, axis=0, keepdims=True)
    delta = jnp.sum(dot_sum, axis=0, keepdims=True) * inverse

    for head in range(GROUP):
        part = slice(head * tok_rows, (head + 1) * tok_rows)
        scale = jnp.broadcast_to(inverse[:, part], (HD, tok_rows)).T
        query_rows[part, :] = (query_rows[part, :].astype(jnp.float32) * (scale * soft_scale)).astype(jnp.bfloat16)
        cot_rows[part, :] = (cot_rows[part, :].astype(jnp.float32) * scale).astype(jnp.bfloat16)

    dqt_ref[...] = jnp.zeros_like(dqt_ref)

    def grad_step(tile, nothing):
        weights = weight_ref[slot(tile), :]
        grad_scores = (
            weights.astype(jnp.float32) * (score_ref[slot(tile), :] - delta)
        ).astype(jnp.bfloat16)
        dkv_ref[at(tile), HD:] = jnp.dot(
            weights, cot_rows[...], preferred_element_type=jnp.float32
        ).astype(jnp.bfloat16)
        dkv_ref[at(tile), :HD] = jnp.dot(
            grad_scores, query_rows[...], preferred_element_type=jnp.float32
        ).astype(jnp.bfloat16)
        dqt_ref[...] += jnp.dot(
            kv_ref[at(tile), :HD].T, grad_scores, preferred_element_type=jnp.float32
        )
        return nothing

    lax.fori_loop(low, high, grad_step, 0)

    def clear(tile, nothing):
        dkv_ref[at(tile), :] = jnp.zeros((TILE, 2 * HD), jnp.bfloat16)
        return nothing

    lax.fori_loop(0, low, clear, 0)
    lax.fori_loop(high, key_tiles, clear, 0)

    for _, piece_out, number, index in blocks:
        piece_out[number] = dkv_ref[block_at(index), :]

    out_scale = inverse * soft_scale
    for head in range(GROUP):
        part = slice(head * tok_rows, (head + 1) * tok_rows)
        dq_ref[:, head * HD:(head + 1) * HD] = (dqt_ref[:, part] * out_scale[:, part]).T.astype(jnp.bfloat16)


def attention(marks, pos, first, queries, grad_out, pieces, tok_rows, first_head, heads_here):
    rows = GROUP * tok_rows
    keys = (BACK + 1) * PLANE * tok_rows
    slots = (DOC_MOST + tok_rows + 2 * TILE - 2) // TILE * TILE
    wide = GROUP * HD
    flops = heads_here * 5 * 2 * rows * DOC_MOST * HD
    piece_specs = [
        pl.BlockSpec((piece.shape[0], tok_rows, 2 * HD), lambda h, marks: (0, 0, h)) for piece in pieces
    ]
    out = pl.pallas_call(
        functools.partial(attention_kernel, tok_rows, keys // TILE),
        grid_spec=pltpu.PrefetchScalarGridSpec(
            num_scalar_prefetch=1,
            grid=(heads_here,),
            in_specs=[
                pl.BlockSpec((1, rows), lambda h, marks: (0, 0)),
                pl.BlockSpec((1, rows), lambda h, marks: (0, 0)),
                pl.BlockSpec((tok_rows, wide), lambda h, marks: (0, first_head + h)),
                pl.BlockSpec((tok_rows, wide), lambda h, marks: (0, first_head + h)),
            ] + piece_specs,
            out_specs=[pl.BlockSpec((tok_rows, wide), lambda h, marks: (0, h))] + piece_specs,
            scratch_shapes=[
                pltpu.VMEM((rows, HD), jnp.bfloat16),
                pltpu.VMEM((rows, HD), jnp.bfloat16),
                pltpu.VMEM((slots, rows), jnp.float32),
                pltpu.VMEM((slots, rows), jnp.bfloat16),
                pltpu.VMEM((HD, rows), jnp.float32),
                pltpu.VMEM((keys, 2 * HD), jnp.bfloat16),
                pltpu.VMEM((keys, 2 * HD), jnp.bfloat16),
            ],
        ),
        out_shape=[jax.ShapeDtypeStruct((tok_rows, heads_here * wide), jnp.bfloat16)]
        + [jax.ShapeDtypeStruct(piece.shape, jnp.bfloat16) for piece in pieces],
        compiler_params=pltpu.CompilerParams(
            dimension_semantics=("arbitrary",), vmem_limit_bytes=40 * 1024 * 1024
        ),
        cost_estimate=pl.CostEstimate(
            flops=flops * 2, bytes_accessed=heads_here * 4 * 1024 * 1024, transcendentals=0
        ),
    )(marks, pos, first, queries, grad_out, *pieces)
    return out[0], out[1:]


def swap(value, offset):
    count = lax.axis_size("ctx")
    return lax.ppermute(value, "ctx", [(source, source ^ offset) for source in range(count)])


def move(value, steps):
    count = lax.axis_size("ctx")
    pairs = [(source, source + steps) for source in range(count) if 0 <= source + steps < count]
    if not pairs:
        return jnp.zeros_like(value)
    return lax.ppermute(value, "ctx", pairs)


def after(value, *earlier):
    return lax.optimization_barrier((value, *earlier))[0]


def seen_by(own, offset):
    place = lax.axis_index("ctx") % PLANE
    return jnp.where(place > (place ^ offset), own[:BACK], own[1:])


def gather_far(part):
    own = jnp.stack([move(part, PLANE * (BACK - plane)) for plane in range(BACK)] + [part])
    return own, swap(seen_by(own, 4), 4)


def gather_x(own, y_piece):
    return swap(jnp.concatenate([seen_by(own, 2), y_piece]), 2)


def gather_core(own, y_piece, x_piece):
    return swap(jnp.concatenate([seen_by(own, 1), y_piece, x_piece]), 1)


def widen(value):
    return value.astype(jnp.float32)


def placed(value, offset):
    place = lax.axis_index("ctx") % PLANE
    blank = jnp.zeros_like(value[:1])
    early, late = jnp.concatenate([value, blank]), jnp.concatenate([blank, value])
    return widen(jnp.where(place > (place ^ offset), early, late))


def sum_core(pieces):
    own, y_piece, x_piece, core_piece = pieces
    got = swap(core_piece, 1)
    x_sum = (widen(x_piece) + widen(got[2 * BACK:])).astype(jnp.bfloat16)
    return own, y_piece, x_sum, got


def sum_x(state):
    own, y_piece, x_sum, from_core = state
    got = swap(x_sum, 2)
    y_sum = (widen(y_piece) + widen(from_core[BACK:2 * BACK]) + widen(got[BACK:])).astype(jnp.bfloat16)
    return own, y_sum, from_core, got


def sum_y(state):
    own, y_sum, from_core, from_x = state
    got = swap(y_sum, 4)
    own_sum = widen(own) + placed(from_core[:BACK], 1) + placed(from_x[:BACK], 2) + placed(got, 4)
    return own_sum.astype(jnp.bfloat16)


def sum_far(own_sum):
    total = widen(own_sum[BACK])
    for plane in range(BACK):
        total = total + widen(move(own_sum[plane], -PLANE * (BACK - plane)))
    return total.astype(jnp.bfloat16)


def input_kernel(key_ref, value_ref, key_weight_ref, value_weight_ref, out_ref):
    total = lax.dot_general(key_ref[...], key_weight_ref[...], NT, preferred_element_type=jnp.float32)
    total = total + lax.dot_general(
        value_ref[...], value_weight_ref[...], NT, preferred_element_type=jnp.float32
    )
    out_ref[...] = total.astype(jnp.bfloat16)


def input_gradient(grad_key, grad_value, key_weight, value_weight):
    tok_rows, columns = grad_key.shape
    width = key_weight.shape[0]
    step = 512
    held = pl.BlockSpec((tok_rows, columns), lambda d: (0, 0))
    streamed = pl.BlockSpec((step, columns), lambda d: (d, 0))
    return pl.pallas_call(
        input_kernel,
        grid=(width // step,),
        in_specs=[held, held, streamed, streamed],
        out_specs=pl.BlockSpec((tok_rows, step), lambda d: (0, d)),
        out_shape=jax.ShapeDtypeStruct((tok_rows, width), jnp.bfloat16),
        compiler_params=pltpu.CompilerParams(
            dimension_semantics=("arbitrary",), vmem_limit_bytes=32 * 1024 * 1024
        ),
        cost_estimate=pl.CostEstimate(
            flops=4 * tok_rows * columns * width, bytes_accessed=4 * width * columns, transcendentals=0
        ),
    )(grad_key, grad_value, key_weight, value_weight)


def shards(queries, key_proj, value_proj, grad_out, key_weight, value_weight, doc_start):
    tok_rows = queries.shape[0]
    heads_kv = key_proj.shape[1] // HD
    my_index = lax.axis_index("ctx")
    begin = my_index * tok_rows
    low = doc_start[0] // TILE
    full_low = (doc_start[tok_rows - 1] + TILE - 1) // TILE
    full_high = (begin + 1) // TILE
    high = (begin + tok_rows + TILE - 1) // TILE
    full_low = jnp.minimum(full_low, high)
    full_high = jnp.maximum(full_high, full_low)
    base = (my_index // PLANE - BACK) * PLANE * tok_rows // TILE
    marks = jnp.stack(
        [low - base, full_low - base, full_high - base, high - base, base, my_index % PLANE]
    ).astype(jnp.int32)
    pos = jnp.tile(begin + jnp.arange(tok_rows, dtype=jnp.int32), GROUP)[None]
    first = jnp.tile(doc_start, GROUP)[None]

    chunks = min(CHUNKS, heads_kv)
    per = heads_kv // chunks
    pair = jnp.stack(
        [key_proj.reshape(tok_rows, heads_kv, HD), value_proj.reshape(tok_rows, heads_kv, HD)], axis=2
    ).reshape(tok_rows, heads_kv * 2 * HD)
    parts = [pair[:, chunk * per * 2 * HD:(chunk + 1) * per * 2 * HD] for chunk in range(chunks)]
    far = [gather_far(part) for part in parts]
    grad_queries, states, sums, done = [], [], [], []
    stages = (sum_core, sum_x, sum_y)
    for chunk in range(chunks):
        own, y_piece = far[chunk]
        if chunk >= 3:
            y_piece = after(y_piece, done[chunk - 3])
        x_piece = gather_x(own, y_piece)
        if chunk >= 2:
            x_piece = after(x_piece, done[chunk - 2])
        core_piece = gather_core(own, y_piece, x_piece)
        held = []
        for earlier in range(chunk - 1):
            stage = chunk - 2 - earlier
            if stage < len(stages):
                states[earlier] = stages[stage](states[earlier])
                held.append(states[earlier])
        core_piece = after(core_piece, *jax.tree.leaves(held)) if held else core_piece
        dq, partials = attention(
            marks, pos, first, queries, grad_out, (own, y_piece, x_piece, core_piece), tok_rows, chunk * per, per
        )
        done.append(dq)
        grad_queries.append(dq)
        states.append(tuple(partials))
    for chunk in range(chunks):
        state = states[chunk]
        for stage in stages[max(0, chunks - 2 - chunk + 0) if chunk < chunks - 1 else 0:]:
            state = stage(state)
        sums.append(sum_far(state))
    grad_query = jnp.concatenate(grad_queries, axis=1)
    both = jnp.concatenate(sums, axis=1).reshape(tok_rows, heads_kv, 2, HD)
    grad_key = both[:, :, 0].reshape(tok_rows, heads_kv * HD)
    grad_value = both[:, :, 1].reshape(tok_rows, heads_kv * HD)
    partial_input = input_gradient(grad_key, grad_value, key_weight, value_weight)
    grad_input = lax.psum_scatter(
        partial_input, "tp", scatter_dimension=1, tiled=True
    )
    return (grad_query, grad_key, grad_value, grad_input)


def solution(mesh):
    in_specs = (
        P("ctx", "tp"),
        P("ctx", "tp"),
        P("ctx", "tp"),
        P("ctx", "tp"),
        P(None, "tp"),
        P(None, "tp"),
        P("ctx"),
    )
    out_specs = (P("ctx", "tp"), P("ctx", "tp"), P("ctx", "tp"), P("ctx", "tp"))
    return jax.shard_map(shards, mesh=mesh, in_specs=in_specs, out_specs=out_specs, check_vma=False)
```

```python
import functools
import math

import jax
import jax.numpy as jnp
from jax import lax
from jax.experimental import pallas as pl
from jax.experimental.pallas import tpu as pltpu
from jax.sharding import PartitionSpec as P

HEADS = 64
KV_HEADS = 8
HD = 128
GROUP = HEADS // KV_HEADS
DOC_MOST = 2048
TILE = 256
CHUNKS = 4
PLANE = 8
BACK = 2

NEGATIVE = -1e30
NT = (((1,), (1,)), ((), ()))


def attention_kernel(
    tok_rows, key_tiles, marks, pos_ref, first_ref, query_ref, cot_ref, own_in, y_in, x_in, core_in,
    dq_ref, own_out, y_out, x_out, core_out,
    query_rows, cot_rows, score_ref, weight_ref, dqt_ref, kv_ref, dkv_ref,
):
    rows = GROUP * tok_rows
    soft_scale = 1.0 / math.sqrt(HD)
    exp2_scale = soft_scale * math.log2(math.e)
    low, full_low, full_high, high = marks[0], marks[1], marks[2], marks[3]
    base, place = marks[4], marks[5]

    blocks = [(own_in, own_out, plane, plane * PLANE + place) for plane in range(BACK + 1)]
    for piece_in, piece_out, offsets in (
        (y_in, y_out, (4,)), (x_in, x_out, (2, 6)), (core_in, core_out, (1, 5, 3, 7))
    ):
        for number, offset in enumerate(offsets):
            source = place ^ offset
            first_plane = jnp.where(source > place, 0, 1)
            for plane in range(BACK):
                blocks.append(
                    (piece_in, piece_out, number * BACK + plane, (first_plane + plane) * PLANE + source)
                )

    def block_at(index):
        return pl.ds(pl.multiple_of(index * tok_rows, tok_rows), tok_rows)

    @pl.when(pl.program_id(0) == 0)
    def _():
        kv_ref[...] = jnp.zeros_like(kv_ref)

    for piece_in, _, number, index in blocks:
        kv_ref[block_at(index), :] = piece_in[number]

    for head in range(GROUP):
        query_rows[head * tok_rows:(head + 1) * tok_rows, :] = query_ref[:, head * HD:(head + 1) * HD]
        cot_rows[head * tok_rows:(head + 1) * tok_rows, :] = cot_ref[:, head * HD:(head + 1) * HD]

    def fold(values):
        return values.reshape(TILE // 8, 8, rows)

    def at(tile):
        return pl.ds(pl.multiple_of(tile * TILE, TILE), TILE)

    def slot(tile):
        return pl.ds(pl.multiple_of((tile - low) * TILE, TILE), TILE)

    def score_step(masked, tile, rowmax):
        scores = lax.dot_general(
            kv_ref[at(tile), :HD], query_rows[...], NT, preferred_element_type=jnp.float32
        )
        if masked:
            key_pos = (base + tile) * TILE + lax.broadcasted_iota(jnp.int32, (TILE, rows), 0)
            visible = (key_pos <= pos_ref[...]) & (key_pos >= first_ref[...])
            scores = jnp.where(visible, scores, NEGATIVE)
        score_ref[slot(tile), :] = scores
        return jnp.maximum(rowmax, jnp.max(fold(scores), axis=0))

    rowmax = jnp.full((8, rows), NEGATIVE, jnp.float32)
    rowmax = lax.fori_loop(low, full_low, functools.partial(score_step, True), rowmax)
    rowmax = lax.fori_loop(full_low, full_high, functools.partial(score_step, False), rowmax)
    rowmax = lax.fori_loop(full_high, high, functools.partial(score_step, True), rowmax)
    shift = jnp.max(rowmax, axis=0, keepdims=True) * exp2_scale

    def weight_step(tile, sums):
        total, dot_sum = sums
        weights = jnp.exp2(score_ref[slot(tile), :] * exp2_scale - shift)
        grad_probs = lax.dot_general(
            kv_ref[at(tile), HD:], cot_rows[...], NT, preferred_element_type=jnp.float32
        )
        weight_ref[slot(tile), :] = weights.astype(jnp.bfloat16)
        score_ref[slot(tile), :] = grad_probs
        total = total + jnp.sum(fold(weights), axis=0)
        dot_sum = dot_sum + jnp.sum(fold(weights * grad_probs), axis=0)
        return (total, dot_sum)

    zeros = jnp.zeros((8, rows), jnp.float32)
    total, dot_sum = lax.fori_loop(low, high, weight_step, (zeros, zeros))
    inverse = 1.0 / jnp.sum(total, axis=0, keepdims=True)
    delta = jnp.sum(dot_sum, axis=0, keepdims=True) * inverse

    for head in range(GROUP):
        part = slice(head * tok_rows, (head + 1) * tok_rows)
        scale = jnp.broadcast_to(inverse[:, part], (HD, tok_rows)).T
        query_rows[part, :] = (query_rows[part, :].astype(jnp.float32) * (scale * soft_scale)).astype(jnp.bfloat16)
        cot_rows[part, :] = (cot_rows[part, :].astype(jnp.float32) * scale).astype(jnp.bfloat16)

    dqt_ref[...] = jnp.zeros_like(dqt_ref)

    def grad_step(tile, nothing):
        weights = weight_ref[slot(tile), :]
        grad_scores = (
            weights.astype(jnp.float32) * (score_ref[slot(tile), :] - delta)
        ).astype(jnp.bfloat16)
        dkv_ref[at(tile), HD:] = jnp.dot(
            weights, cot_rows[...], preferred_element_type=jnp.float32
        ).astype(jnp.bfloat16)
        dkv_ref[at(tile), :HD] = jnp.dot(
            grad_scores, query_rows[...], preferred_element_type=jnp.float32
        ).astype(jnp.bfloat16)
        dqt_ref[...] += jnp.dot(
            kv_ref[at(tile), :HD].T, grad_scores, preferred_element_type=jnp.float32
        )
        return nothing

    lax.fori_loop(low, high, grad_step, 0)

    def clear(tile, nothing):
        dkv_ref[at(tile), :] = jnp.zeros((TILE, 2 * HD), jnp.bfloat16)
        return nothing

    lax.fori_loop(0, low, clear, 0)
    lax.fori_loop(high, key_tiles, clear, 0)

    for _, piece_out, number, index in blocks:
        piece_out[number] = dkv_ref[block_at(index), :]

    out_scale = inverse * soft_scale
    for head in range(GROUP):
        part = slice(head * tok_rows, (head + 1) * tok_rows)
        dq_ref[:, head * HD:(head + 1) * HD] = (dqt_ref[:, part] * out_scale[:, part]).T.astype(jnp.bfloat16)


def attention(marks, pos, first, queries, grad_out, pieces, tok_rows, first_head, heads_here):
    rows = GROUP * tok_rows
    keys = (BACK + 1) * PLANE * tok_rows
    slots = (DOC_MOST + tok_rows + 2 * TILE - 2) // TILE * TILE
    wide = GROUP * HD
    flops = heads_here * 5 * 2 * rows * DOC_MOST * HD
    piece_specs = [
        pl.BlockSpec((piece.shape[0], tok_rows, 2 * HD), lambda h, marks: (0, 0, h)) for piece in pieces
    ]
    out = pl.pallas_call(
        functools.partial(attention_kernel, tok_rows, keys // TILE),
        grid_spec=pltpu.PrefetchScalarGridSpec(
            num_scalar_prefetch=1,
            grid=(heads_here,),
            in_specs=[
                pl.BlockSpec((1, rows), lambda h, marks: (0, 0)),
                pl.BlockSpec((1, rows), lambda h, marks: (0, 0)),
                pl.BlockSpec((tok_rows, wide), lambda h, marks: (0, first_head + h)),
                pl.BlockSpec((tok_rows, wide), lambda h, marks: (0, first_head + h)),
            ] + piece_specs,
            out_specs=[pl.BlockSpec((tok_rows, wide), lambda h, marks: (0, h))] + piece_specs,
            scratch_shapes=[
                pltpu.VMEM((rows, HD), jnp.bfloat16),
                pltpu.VMEM((rows, HD), jnp.bfloat16),
                pltpu.VMEM((slots, rows), jnp.float32),
                pltpu.VMEM((slots, rows), jnp.bfloat16),
                pltpu.VMEM((HD, rows), jnp.float32),
                pltpu.VMEM((keys, 2 * HD), jnp.bfloat16),
                pltpu.VMEM((keys, 2 * HD), jnp.bfloat16),
            ],
        ),
        out_shape=[jax.ShapeDtypeStruct((tok_rows, heads_here * wide), jnp.bfloat16)]
        + [jax.ShapeDtypeStruct(piece.shape, jnp.bfloat16) for piece in pieces],
        compiler_params=pltpu.CompilerParams(
            dimension_semantics=("arbitrary",), vmem_limit_bytes=40 * 1024 * 1024
        ),
        cost_estimate=pl.CostEstimate(
            flops=flops * 2, bytes_accessed=heads_here * 4 * 1024 * 1024, transcendentals=0
        ),
    )(marks, pos, first, queries, grad_out, *pieces)
    return out[0], out[1:]


def swap(value, offset):
    count = lax.axis_size("ctx")
    return lax.ppermute(value, "ctx", [(source, source ^ offset) for source in range(count)])


def move(value, steps):
    count = lax.axis_size("ctx")
    pairs = [(source, source + steps) for source in range(count) if 0 <= source + steps < count]
    if not pairs:
        return jnp.zeros_like(value)
    return lax.ppermute(value, "ctx", pairs)


def after(value, *earlier):
    return lax.optimization_barrier((value, *earlier))[0]


def seen_by(own, offset):
    place = lax.axis_index("ctx") % PLANE
    return jnp.where(place > (place ^ offset), own[:BACK], own[1:])


def gather_far(part):
    own = jnp.stack([move(part, PLANE * (BACK - plane)) for plane in range(BACK)] + [part])
    return own, swap(seen_by(own, 4), 4)


def gather_x(own, y_piece):
    return swap(jnp.concatenate([seen_by(own, 2), y_piece]), 2)


def gather_core(own, y_piece, x_piece):
    return swap(jnp.concatenate([seen_by(own, 1), y_piece, x_piece]), 1)


def widen(value):
    return value.astype(jnp.float32)


def placed(value, offset):
    place = lax.axis_index("ctx") % PLANE
    blank = jnp.zeros_like(value[:1])
    early, late = jnp.concatenate([value, blank]), jnp.concatenate([blank, value])
    return widen(jnp.where(place > (place ^ offset), early, late))


def sum_core(pieces):
    own, y_piece, x_piece, core_piece = pieces
    got = swap(core_piece, 1)
    x_sum = (widen(x_piece) + widen(got[2 * BACK:])).astype(jnp.bfloat16)
    return own, y_piece, x_sum, got


def sum_x(state):
    own, y_piece, x_sum, from_core = state
    got = swap(x_sum, 2)
    y_sum = (widen(y_piece) + widen(from_core[BACK:2 * BACK]) + widen(got[BACK:])).astype(jnp.bfloat16)
    return own, y_sum, from_core, got


def sum_y(state):
    own, y_sum, from_core, from_x = state
    got = swap(y_sum, 4)
    own_sum = widen(own) + placed(from_core[:BACK], 1) + placed(from_x[:BACK], 2) + placed(got, 4)
    return own_sum.astype(jnp.bfloat16)


def sum_far(own_sum):
    total = widen(own_sum[BACK])
    for plane in range(BACK):
        total = total + widen(move(own_sum[plane], -PLANE * (BACK - plane)))
    return total.astype(jnp.bfloat16)


def input_kernel(key_ref, value_ref, key_weight_ref, value_weight_ref, out_ref):
    total = lax.dot_general(key_ref[...], key_weight_ref[...], NT, preferred_element_type=jnp.float32)
    total = total + lax.dot_general(
        value_ref[...], value_weight_ref[...], NT, preferred_element_type=jnp.float32
    )
    out_ref[...] = total.astype(jnp.bfloat16)


def input_gradient(grad_key, grad_value, key_weight, value_weight):
    tok_rows, columns = grad_key.shape
    width = key_weight.shape[0]
    step = 512
    held = pl.BlockSpec((tok_rows, columns), lambda d: (0, 0))
    streamed = pl.BlockSpec((step, columns), lambda d: (d, 0))
    return pl.pallas_call(
        input_kernel,
        grid=(width // step,),
        in_specs=[held, held, streamed, streamed],
        out_specs=pl.BlockSpec((tok_rows, step), lambda d: (0, d)),
        out_shape=jax.ShapeDtypeStruct((tok_rows, width), jnp.bfloat16),
        compiler_params=pltpu.CompilerParams(
            dimension_semantics=("arbitrary",), vmem_limit_bytes=32 * 1024 * 1024
        ),
        cost_estimate=pl.CostEstimate(
            flops=4 * tok_rows * columns * width, bytes_accessed=4 * width * columns, transcendentals=0
        ),
    )(grad_key, grad_value, key_weight, value_weight)


def shards(queries, key_proj, value_proj, grad_out, key_weight, value_weight, doc_start):
    tok_rows = queries.shape[0]
    heads_kv = key_proj.shape[1] // HD
    my_index = lax.axis_index("ctx")
    begin = my_index * tok_rows
    low = doc_start[0] // TILE
    full_low = (doc_start[tok_rows - 1] + TILE - 1) // TILE
    full_high = (begin + 1) // TILE
    high = (begin + tok_rows + TILE - 1) // TILE
    full_low = jnp.minimum(full_low, high)
    full_high = jnp.maximum(full_high, full_low)
    base = (my_index // PLANE - BACK) * PLANE * tok_rows // TILE
    marks = jnp.stack(
        [low - base, full_low - base, full_high - base, high - base, base, my_index % PLANE]
    ).astype(jnp.int32)
    pos = jnp.tile(begin + jnp.arange(tok_rows, dtype=jnp.int32), GROUP)[None]
    first = jnp.tile(doc_start, GROUP)[None]

    chunks = min(CHUNKS, heads_kv)
    per = heads_kv // chunks
    pair = jnp.stack(
        [key_proj.reshape(tok_rows, heads_kv, HD), value_proj.reshape(tok_rows, heads_kv, HD)], axis=2
    ).reshape(tok_rows, heads_kv * 2 * HD)
    parts = [pair[:, chunk * per * 2 * HD:(chunk + 1) * per * 2 * HD] for chunk in range(chunks)]
    far = [gather_far(parts[0])]
    first_x = gather_x(*far[0])
    far += [
        gather_far(after(part, far[0][1] if chunk == 0 else first_x)) for chunk, part in enumerate(parts[1:])
    ]
    grad_queries, states, sums, done = [], [], [], []
    stages = (sum_core, sum_x, sum_y)
    for chunk in range(chunks):
        own, y_piece = far[chunk]
        if chunk >= 3:
            y_piece = after(y_piece, done[chunk - 3])
        x_piece = gather_x(own, y_piece) if chunk else first_x
        if chunk >= 2:
            x_piece = after(x_piece, done[chunk - 2])
        core_piece = gather_core(own, y_piece, x_piece)
        held = []
        for earlier in range(chunk - 1):
            stage = chunk - 2 - earlier
            if stage < len(stages):
                states[earlier] = stages[stage](states[earlier])
                held.append(states[earlier])
        core_piece = after(core_piece, *jax.tree.leaves(held)) if held else core_piece
        dq, partials = attention(
            marks, pos, first, queries, grad_out, (own, y_piece, x_piece, core_piece), tok_rows, chunk * per, per
        )
        done.append(dq)
        grad_queries.append(dq)
        states.append(tuple(partials))
    for chunk in range(chunks):
        state = states[chunk]
        for stage in stages[max(0, chunks - 2 - chunk + 0) if chunk < chunks - 1 else 0:]:
            state = stage(state)
        sums.append(sum_far(state))
    grad_query = jnp.concatenate(grad_queries, axis=1)
    both = jnp.concatenate(sums, axis=1).reshape(tok_rows, heads_kv, 2, HD)
    grad_key = both[:, :, 0].reshape(tok_rows, heads_kv * HD)
    grad_value = both[:, :, 1].reshape(tok_rows, heads_kv * HD)
    partial_input = input_gradient(grad_key, grad_value, key_weight, value_weight)
    grad_input = lax.psum_scatter(
        partial_input, "tp", scatter_dimension=1, tiled=True
    )
    return (grad_query, grad_key, grad_value, grad_input)


def solution(mesh):
    in_specs = (
        P("ctx", "tp"),
        P("ctx", "tp"),
        P("ctx", "tp"),
        P("ctx", "tp"),
        P(None, "tp"),
        P(None, "tp"),
        P("ctx"),
    )
    out_specs = (P("ctx", "tp"), P("ctx", "tp"), P("ctx", "tp"), P("ctx", "tp"))
    return jax.shard_map(shards, mesh=mesh, in_specs=in_specs, out_specs=out_specs, check_vma=False)
```
